32 devices in a mesh: dp: 8 (over y, x, core), seq: 4 (over z).
Axes of the slice: x: 2, y: 2, z: 4, core: 2. Of those that a mesh axis runs over, the one named last changes fastest.
Arguments:
- tokens: bfloat16 [2, 16, 608, 1024], P(None, 'dp', 'seq'), may hold values from -6 to 6
- pad_mask: int32 [2, 16, 608], P(None, 'dp', 'seq'), may hold values from 0 to 1, as said below
- image_counts: int32 [2, 8], P(None, 'dp'), may hold values from 1 to 2, as said below
- cotangent: bfloat16 [2, 16, 608, 1024], P(None, 'dp', 'seq'), may hold values from -6 to 6
- gain_one: bfloat16 [1024], P(('dp', 'seq')), may hold values from 0.099609375 to 1.8984375
- shift_one: bfloat16 [1024], P(('dp', 'seq')), may hold values from -3 to 3
- qkv_weight: bfloat16 [1024, 3072], P(('dp', 'seq')), may hold values from -0.1875 to 0.1875
- query_bias: bfloat16 [1024], P(('dp', 'seq')), may hold values from -3 to 3
- value_bias: bfloat16 [1024], P(('dp', 'seq')), may hold values from -6 to 6
- out_weight: bfloat16 [1024, 1024], P(('dp', 'seq')), may hold values from -1 to 1
- out_bias: bfloat16 [1024], P(('dp', 'seq')), may hold values from -3 to 3
- gain_two: bfloat16 [1024], P(('dp', 'seq')), may hold values from 0.099609375 to 1.8984375
- shift_two: bfloat16 [1024], P(('dp', 'seq')), may hold values from -3 to 3
- up_weight: bfloat16 [1024, 4096], P(('dp', 'seq')), may hold values from -0.1875 to 0.1875
- up_bias: bfloat16 [4096], P(('dp', 'seq')), may hold values from -3 to 3
- down_weight: bfloat16 [4096, 1024], P(('dp', 'seq')), may hold values from -0.09375 to 0.09375
- down_bias: bfloat16 [1024], P(('dp', 'seq')), may hold values from -3 to 3
Outputs:
- block_out: bfloat16 [2, 16, 608, 1024], P(None, 'dp', 'seq')
- grad_tokens: float32 [2, 16, 608, 1024], P(None, 'dp', 'seq')
- grad_gain_one: float32 [1024], P(('dp', 'seq'))
- grad_shift_one: float32 [1024], P(('dp', 'seq'))
- grad_qkv_weight: float32 [1024, 3072], P(('dp', 'seq'))
- grad_query_bias: float32 [1024], P(('dp', 'seq'))
- grad_value_bias: float32 [1024], P(('dp', 'seq'))
- grad_out_weight: float32 [1024, 1024], P(('dp', 'seq'))
- grad_out_bias: float32 [1024], P(('dp', 'seq'))
- grad_gain_two: float32 [1024], P(('dp', 'seq'))
- grad_shift_two: float32 [1024], P(('dp', 'seq'))
- grad_up_weight: float32 [1024, 4096], P(('dp', 'seq'))
- grad_up_bias: float32 [4096], P(('dp', 'seq'))
- grad_down_weight: float32 [4096, 1024], P(('dp', 'seq'))
- grad_down_bias: float32 [1024], P(('dp', 'seq'))
The draws below stay inside these ranges and needn't reach their ends.
Inputs may be any that keep to these rules, and one draw needn't show every extreme that they name: `pad_mask`: each image's mask is 1 on its first tokens and 0 after them; more than 456 tokens of every image are 1, at most min(577, 608), and some image has exactly that many. `image_counts`: some entry is 2 and some entry is 1.
All inputs are finite; a program needn't handle non-finite values.
Results may differ from the reference program's by a relative error of at most 0.012.
Values may be sent and summed in bfloat16 or wider, within the bound.
A program may use at most 256 MiB of HBM per device.

```python
import jax
import jax.numpy as jnp
from jax import lax

D = 1024
HEADS = 16
HEAD_DIM = 64
FF = 4096
SLOTS = 2
SEQ_DEV = 152
MB = 2
TOK_IMG = 577
LEN = 608
IMAGES = 16
NUM_GROUPS = 8


def draw_pad_mask(key, part):
    key = jax.random.fold_in(key, 11)
    low_end = LEN - SEQ_DEV + 1
    high_end = min(TOK_IMG, LEN)
    first_key, second_key = jax.random.split(key)
    lengths = jax.random.randint(first_key, (MB * IMAGES,), low_end, high_end + 1)
    chosen = jax.random.randint(second_key, (), 0, MB * IMAGES)
    lengths = lengths.at[chosen].set(high_end)
    places = jnp.arange(LEN, dtype=jnp.int32)
    return (places[None, :] < lengths[:, None]).astype(jnp.int32).reshape(MB, IMAGES, LEN)


def draw_image_counts(key, part):
    key = jax.random.fold_in(key, 23)
    first_key, second_key = jax.random.split(key)
    count_table = jax.random.randint(first_key, (MB * NUM_GROUPS,), 1, SLOTS + 1)
    chosen = jax.random.randint(second_key, (), 0, MB * NUM_GROUPS)
    count_table = count_table.at[chosen].set(SLOTS)
    count_table = count_table.at[(chosen + 1) % (MB * NUM_GROUPS)].set(1)
    return count_table.reshape(MB, NUM_GROUPS).astype(jnp.int32)


def spiked(entries, stream_key, source, target, parts, factor):
    def block_of(axis_at):
        return (jnp.arange(entries.shape[axis_at]) // (entries.shape[axis_at] // parts)).reshape((-1,) + (1,) * (entries.ndim - 1 - axis_at))

    near = jax.random.permutation(stream_key, parts)[block_of(target)]
    other_side = (block_of(target) + parts // 2) % parts
    return jnp.where((block_of(source) == near) | (block_of(source) == other_side), factor * entries, entries)


def block_scale(stream_key, extent, shards, smallest, largest):
    loudness = 1.0
    for position, parts in shards:
        heights = jax.random.uniform(jax.random.fold_in(jax.random.fold_in(stream_key, 6), position), (parts,), jnp.float32, smallest / len(shards), largest / len(shards))
        loudness = loudness * jnp.repeat(jnp.exp(heights), extent[position] // parts).reshape((-1,) + (1,) * (len(extent) - 1 - position))
    return loudness


def noise(own_key, dims, deviation, reach, pieces=(), kind=jnp.bfloat16):
    values = jax.random.normal(own_key, dims, jnp.float32) * deviation
    if len(pieces) > 0:
        values = block_scale(own_key, dims, pieces, -0.22, 0.18) * values
    return jnp.clip(values, min=-reach, max=reach).astype(kind)


def noise_with(stream_key, shape, scale, reach, pieces, heavy, kind=jnp.bfloat16):
    values = scale * jax.random.normal(stream_key, shape, jnp.float32)
    if pieces:
        values = values * block_scale(stream_key, shape, pieces, -0.22, 0.18)
    return jnp.clip(spiked(values, jax.random.fold_in(stream_key, 3), *heavy), -reach, reach).astype(kind)


def setup_inputs(seed: int = 0) -> dict:
    keys = jax.random.split(jax.random.key(seed), 18)
    return {
        "tokens": noise(keys[0], (MB, IMAGES, LEN, D), 1.0, 6.0, ((1, 8), (2, 4))),
        "pad_mask": draw_pad_mask(jax.random.fold_in(keys[17], 71), 0),
        "image_counts": draw_image_counts(jax.random.fold_in(keys[17], 71), 0),
        "cotangent": noise_with(keys[3], (MB, IMAGES, LEN, D), 1.0, 6.0, ((1, 8), (2, 4)), (1, 3, 8, 2.0)),
        "gain_one": jnp.clip(1.0 + 0.18 * jax.random.normal(keys[4], (D,), jnp.float32), 0.099609375, 1.8984375).astype(jnp.bfloat16),
        "shift_one": noise(keys[5], (D,), 0.5, 3.0, ((0, 32),)),
        "qkv_weight": noise(keys[6], (D, 3 * D), D ** -0.5, 0.1875, ((0, 32),)),
        "query_bias": noise(keys[7], (D,), 0.5, 3.0, ((0, 32),)),
        "value_bias": noise(keys[8], (D,), 1.0, 6.0, ((0, 32),)),
        "out_weight": noise(keys[9], (D, D), (D // 32) ** -0.5, 1.0, ((0, 32),)),
        "out_bias": noise(keys[10], (D,), 0.5, 3.0, ((0, 32),)),
        "gain_two": jnp.clip(1.0 + 0.18 * jax.random.normal(keys[11], (D,), jnp.float32), 0.099609375, 1.8984375).astype(jnp.bfloat16),
        "shift_two": noise(keys[12], (D,), 0.5, 3.0, ((0, 32),)),
        "up_weight": noise(keys[13], (D, FF), D ** -0.5, 0.1875, ((0, 32),)),
        "up_bias": noise(keys[14], (FF,), 0.5, 3.0, ((0, 32),)),
        "down_weight": noise(keys[15], (FF, D), FF ** -0.5, 0.09375, ((0, 32),)),
        "down_bias": noise(keys[16], (D,), 0.5, 3.0, ((0, 32),)),
    }


@jax.custom_vjp
def low(v):
    return lax.optimization_barrier(v.astype(jnp.bfloat16)).astype(jnp.float32)

@jax.custom_vjp
def low_back(v):
    return v

def low_keep(v):
    return (low(v), None)

def low_pass(kept, grad):
    return (grad,)

def back_keep(v):
    return (v, None)

def back_low(kept, grad):
    return (low(grad),)
low.defvjp(low_keep, low_pass)
low_back.defvjp(back_keep, back_low)
EPSILON = 1e-06
MASKED = -1e+30

def norm_rows(values, gain_vec, shift_vec):
    center = values - lax.optimization_barrier(jnp.mean(values, -1, keepdims=True))
    spread = lax.optimization_barrier(jnp.mean(center * center, -1, keepdims=True))
    return center * lax.rsqrt(spread + EPSILON) * gain_vec + shift_vec

def product(left_side, right_side):
    return jnp.dot(left_side, right_side, precision=lax.Precision.HIGHEST, preferred_element_type=jnp.float32)

def forward(params, image_rows, image_okay):
    gain_one, shift_one, qkv_weight, query_bias, value_bias, out_weight, out_bias, gain_two, shift_two, up_weight, up_bias, down_weight, down_bias = params
    normed_one = low(norm_rows(image_rows, gain_one, shift_one))
    qkv_mixed = product(normed_one, qkv_weight)
    queries = low(low_back((qkv_mixed[:, :D] + query_bias) * HEAD_DIM ** (-0.5)))
    key_rows = low(low_back(qkv_mixed[:, D:2 * D]))
    value_rows = low(low_back(qkv_mixed[:, 2 * D:] + value_bias))
    query_heads = queries.reshape(LEN, HEADS, HEAD_DIM)
    key_heads = key_rows.reshape(LEN, HEADS, HEAD_DIM)
    value_heads = value_rows.reshape(LEN, HEADS, HEAD_DIM)
    scores = low_back(jnp.einsum('qhd,khd->hqk', query_heads, key_heads, precision=lax.Precision.HIGHEST))
    scores = jnp.where(image_okay[None, None, :] > 0, scores, MASKED)
    row_top = lax.optimization_barrier(jnp.max(scores, -1, keepdims=True))
    exp_scores = jnp.exp(scores - row_top)
    attn_probs = low(exp_scores / lax.optimization_barrier(jnp.sum(exp_scores, -1, keepdims=True)))
    attended = jnp.einsum('hqk,khd->qhd', attn_probs, value_heads, precision=lax.Precision.HIGHEST)
    attended = low(low_back(attended.reshape(LEN, D)))
    branch_one = low_back(product(attended, out_weight) + out_bias)
    middle = image_rows + branch_one
    normed_two = low(norm_rows(middle, gain_two, shift_two))
    pre_act = low_back(product(normed_two, up_weight) + up_bias)
    hidden = low(jax.nn.gelu(pre_act, approximate=False))
    branch_two = low_back(product(hidden, down_weight) + down_bias)
    return middle + branch_two

def reference(tokens, pad_mask, image_counts, cotangent, gain_one, shift_one, qkv_weight, query_bias, value_bias, out_weight, out_bias, gain_two, shift_two, up_weight, up_bias, down_weight, down_bias):
    params = tuple((member.astype(jnp.float32) for member in (gain_one, shift_one, qkv_weight, query_bias, value_bias, out_weight, out_bias, gain_two, shift_two, up_weight, up_bias, down_weight, down_bias)))
    slot_index = jnp.arange(IMAGES, dtype=jnp.int32) % SLOTS
    slot_live = (slot_index[None, :] < jnp.repeat(image_counts, SLOTS, axis=1)).astype(jnp.float32)
    live_rows = pad_mask.astype(jnp.float32) * slot_live[:, :, None]
    flat_tokens = tokens.astype(jnp.float32).reshape(MB * IMAGES, LEN, D)
    flat_grads = (cotangent.astype(jnp.float32) * live_rows[..., None]).reshape(MB * IMAGES, LEN, D)
    flat_okay = pad_mask.reshape(MB * IMAGES, LEN)

    def one_image(totals, items):
        image_rows, image_grad, image_okay = items
        result, pullback = jax.vjp(lambda param_set, rows_in: forward(param_set, rows_in, image_okay), params, image_rows)
        param_grads, input_grad = pullback(image_grad)
        totals = tuple((total + added for total, added in zip(totals, param_grads)))
        return (totals, (result.astype(jnp.bfloat16), input_grad))
    zero_grads = tuple((jnp.zeros(member.shape, jnp.float32) for member in params))
    totals, (results, input_grads) = lax.scan(one_image, zero_grads, (flat_tokens, flat_grads, flat_okay))
    return (results.reshape(MB, IMAGES, LEN, D), input_grads.reshape(MB, IMAGES, LEN, D), totals[0], totals[1], totals[2], totals[3], totals[4], totals[5], totals[6], totals[7], totals[8], totals[9], totals[10], totals[11], totals[12])
```

```python
import jax
import jax.numpy as jnp
from jax import lax
from jax.sharding import PartitionSpec as P

HEADS = 16


EPSILON = 1e-06
MASKED = -1e30
BOTH = ("dp", "seq")
BF16 = jnp.bfloat16
F32 = jnp.float32


def norm_stats(values):
    center = values - jnp.mean(values, -1, keepdims=True)
    spread = jnp.mean(center * center, -1, keepdims=True)
    inverse = lax.rsqrt(spread + EPSILON)
    return center * inverse, inverse


def norm_back(grads, gain_vec, unit, inverse):
    scaled = grads * gain_vec
    first = jnp.mean(scaled, -1, keepdims=True)
    second = jnp.mean(scaled * unit, -1, keepdims=True)
    return inverse * (scaled - first - unit * second)


def matmul(left_side, right_side):
    return jnp.dot(left_side, right_side, preferred_element_type=F32)


def matmul_tn(left_side, right_side):
    return lax.dot_general(
        left_side, right_side, (((0,), (0,)), ((), ())), preferred_element_type=F32
    )


def matmul_nt(left_side, right_side):
    return lax.dot_general(
        left_side, right_side, (((1,), (1,)), ((), ())), preferred_element_type=F32
    )


def gather(shard):
    return lax.all_gather(shard, BOTH, axis=0, tiled=True)


def scatter(total):
    return lax.psum_scatter(total.astype(BF16), BOTH, scatter_dimension=0, tiled=True).astype(F32)


def gather_vectors(vectors):
    packed = lax.all_gather(jnp.concatenate(vectors), BOTH, axis=0, tiled=False)
    unpacked = []
    start = 0
    for member in vectors:
        extent = member.shape[0]
        unpacked.append(packed[:, start : start + extent].reshape(-1).astype(F32))
        start += extent
    return unpacked


def scatter_vectors(totals, group_size):
    packed = jnp.concatenate([total.reshape(group_size, -1) for total in totals], 1)
    owned = lax.psum_scatter(packed, BOTH, scatter_dimension=0, tiled=True).reshape(-1)
    pieces = []
    start = 0
    for total in totals:
        extent = total.shape[0] // group_size
        pieces.append(owned[start : start + extent])
        start += extent
    return pieces


def exchange(blocks):
    return lax.all_to_all(blocks, "seq", split_axis=0, concat_axis=0, tiled=True)


def to_images(values):
    seq_size = lax.axis_size("seq")
    tail = values.shape[2:]
    swapped = exchange(values.reshape((-1,) + tail))
    by_source = jnp.swapaxes(swapped.reshape((seq_size, -1) + tail), 0, 1)
    return by_source.reshape((by_source.shape[0], seq_size * tail[0]) + tail[1:])


def to_tokens(values, like):
    seq_size = lax.axis_size("seq")
    tail = like.shape[2:]
    by_target = jnp.swapaxes(values.reshape((-1, seq_size) + tail), 0, 1)
    return exchange(by_target.reshape((-1,) + tail)).reshape(like.shape)


def attention_forward(queries, keys, values, okay):
    images, extent, width = queries.shape
    split = (images, extent, HEADS, width // HEADS)
    scores = jnp.einsum(
        "sqhd,skhd->shqk", queries.reshape(split), keys.reshape(split), preferred_element_type=F32
    )
    scores = jnp.where(okay[:, None, None, :] > 0, scores, MASKED)
    exp_scores = jnp.exp(scores - jnp.max(scores, -1, keepdims=True))
    probs = (exp_scores / jnp.sum(exp_scores, -1, keepdims=True)).astype(BF16)
    attended = jnp.einsum("shqk,skhd->sqhd", probs, values.reshape(split), preferred_element_type=F32)
    return attended.reshape(images, extent, width).astype(BF16), probs


def attention_backward(queries, keys, values, probs, grads):
    images, extent, width = queries.shape
    split = (images, extent, HEADS, width // HEADS)
    grad_heads = grads.reshape(split)
    grad_probs = jnp.einsum(
        "sqhd,skhd->shqk", grad_heads, values.reshape(split), preferred_element_type=F32
    )
    exact = probs.astype(F32)
    inner = jnp.sum(exact * grad_probs, -1, keepdims=True)
    grad_scores = (exact * (grad_probs - inner)).astype(BF16)
    scale = (width // HEADS) ** (-0.5)
    gq = jnp.einsum("shqk,skhd->sqhd", grad_scores, keys.reshape(split), preferred_element_type=F32)
    gk = jnp.einsum("shqk,sqhd->skhd", grad_scores, queries.reshape(split), preferred_element_type=F32)
    gv = jnp.einsum("shqk,sqhd->skhd", probs, grad_heads, preferred_element_type=F32)
    shape = (images * extent, width)
    return (
        (gq.astype(BF16) * scale).reshape(shape),
        gk.astype(BF16).reshape(shape),
        gv.astype(BF16).reshape(shape),
    )


def on_device(
    tokens,
    pad_mask,
    image_counts,
    cotangent,
    gain_one,
    shift_one,
    qkv_weight,
    query_bias,
    value_bias,
    out_weight,
    out_bias,
    gain_two,
    shift_two,
    up_weight,
    up_bias,
    down_weight,
    down_bias,
):
    micro_count, slot_count, local_len, width = tokens.shape
    seq_size = lax.axis_size("seq")
    group_size = lax.axis_size(BOTH)
    images = micro_count * slot_count // seq_size
    extent = local_len * seq_size
    rows = images * extent
    query_scale = (width // HEADS) ** (-0.5)

    vectors = gather_vectors(
        [
            gain_one,
            shift_one,
            query_bias,
            value_bias,
            out_bias,
            gain_two,
            shift_two,
            up_bias,
            down_bias,
        ]
    )
    gain1, shift1, qbias, vbias, obias, gain2, shift2, ubias, dbias = vectors
    mix_full = gather(qkv_weight)
    proj_full = gather(out_weight)
    up_full = gather(up_weight)
    down_full = gather(down_weight)

    image_okay = to_images(pad_mask)
    image_rows = to_images(tokens)
    image_grad = to_images(cotangent)

    place = lax.axis_index("seq") * images + jnp.arange(images)
    counts = image_counts[place // slot_count, 0]
    live = (image_okay > 0) & ((place % slot_count) < counts)[:, None]

    x = image_rows.reshape(rows, width).astype(F32)
    unit1, inverse1 = norm_stats(x)
    h1 = (unit1 * gain1 + shift1).astype(BF16)
    mixed = matmul(h1, mix_full)
    queries = ((mixed[:, :width] + qbias) * query_scale).astype(BF16)
    keys = mixed[:, width : 2 * width].astype(BF16)
    values = (mixed[:, 2 * width :] + vbias).astype(BF16)
    per_image = (images, extent, width)
    queries, keys, values = (
        queries.reshape(per_image),
        keys.reshape(per_image),
        values.reshape(per_image),
    )
    attended, probs = attention_forward(queries, keys, values, image_okay)
    attended = attended.reshape(rows, width)
    middle = x + (matmul(attended, proj_full) + obias)
    unit2, inverse2 = norm_stats(middle)
    h2 = (unit2 * gain2 + shift2).astype(BF16)
    pre_act = matmul(h2, up_full) + ubias
    hidden = jax.nn.gelu(pre_act, approximate=False).astype(BF16)
    result = (middle + (matmul(hidden, down_full) + dbias)).astype(BF16)
    block_out = to_tokens(result.reshape(per_image), tokens)

    c = jnp.where(live[..., None], image_grad, jnp.zeros_like(image_grad)).reshape(rows, width)
    w_down, c = lax.optimization_barrier((matmul_tn(hidden, c).astype(BF16), c))
    d_down = scatter(w_down)
    d_dbias = jnp.sum(c.astype(F32), 0)
    gelu_slope = jax.vjp(lambda u: jax.nn.gelu(u, approximate=False), pre_act)[1]
    du = gelu_slope(matmul_nt(c, down_full))[0].astype(BF16)
    w_up, du = lax.optimization_barrier((matmul_tn(h2, du).astype(BF16), du))
    d_up = scatter(w_up)
    d_ubias = jnp.sum(du.astype(F32), 0)
    g2 = matmul_nt(du, up_full)
    d_gain2 = jnp.sum(g2 * unit2, 0)
    d_shift2 = jnp.sum(g2, 0)
    gx2 = c.astype(F32) + norm_back(g2, gain2, unit2, inverse2)
    ga = gx2.astype(BF16)
    w_out, ga = lax.optimization_barrier((matmul_tn(attended, ga).astype(BF16), ga))
    d_out = scatter(w_out)
    d_obias = jnp.sum(ga.astype(F32), 0)
    go = matmul_nt(ga, proj_full).astype(BF16).reshape(per_image)
    gq, gk, gv = attention_backward(queries, keys, values, probs, go)
    gz = jnp.concatenate([gq, gk, gv], 1)
    w_mix, gz = lax.optimization_barrier((matmul_tn(h1, gz).astype(BF16), gz))
    d_mix = scatter(w_mix)
    d_qbias = jnp.sum(gq.astype(F32), 0)
    d_vbias = jnp.sum(gv.astype(F32), 0)
    g1 = matmul_nt(gz, mix_full)
    d_gain1 = jnp.sum(g1 * unit1, 0)
    d_shift1 = jnp.sum(g1, 0)
    gx = gx2 + norm_back(g1, gain1, unit1, inverse1)
    grad_tokens = to_tokens(gx.astype(BF16).reshape(per_image), tokens).astype(F32)
    small = scatter_vectors(
        [
            d_gain1,
            d_shift1,
            d_qbias,
            d_vbias,
            d_obias,
            d_gain2,
            d_shift2,
            d_ubias,
            d_dbias,
        ],
        group_size,
    )
    return (
        block_out,
        grad_tokens,
        small[0],
        small[1],
        d_mix,
        small[2],
        small[3],
        d_out,
        small[4],
        small[5],
        small[6],
        d_up,
        small[7],
        d_down,
        small[8],
    )


def solution(mesh):
    image_spec = P(None, "dp", "seq", None)
    vector = P(BOTH)
    matrix = P(BOTH, None)
    params = (
        vector,
        vector,
        matrix,
        vector,
        vector,
        matrix,
        vector,
        vector,
        vector,
        matrix,
        vector,
        matrix,
        vector,
    )
    return jax.shard_map(
        on_device,
        mesh=mesh,
        in_specs=(image_spec, P(None, "dp", "seq"), P(None, "dp"), image_spec) + params,
        out_specs=(image_spec, image_spec) + params,
        check_vma=False,
    )
```

```python
import jax
import jax.numpy as jnp
from jax import lax
from jax.experimental import pallas as pl
from jax.experimental.pallas import tpu as pltpu
from jax.sharding import PartitionSpec as P

HEADS = 16


EPSILON = 1e-06
MASKED = -1e30
BOTH = ("dp", "seq")
BF16 = jnp.bfloat16
F32 = jnp.float32


def norm_stats(values):
    center = values - jnp.mean(values, -1, keepdims=True)
    spread = jnp.mean(center * center, -1, keepdims=True)
    inverse = lax.rsqrt(spread + EPSILON)
    return center * inverse, inverse


def norm_back(grads, gain_vec, unit, inverse):
    scaled = grads * gain_vec
    first = jnp.mean(scaled, -1, keepdims=True)
    second = jnp.mean(scaled * unit, -1, keepdims=True)
    return inverse * (scaled - first - unit * second)


def matmul(left_side, right_side):
    return jnp.dot(left_side, right_side, preferred_element_type=F32)


def matmul_tn(left_side, right_side):
    return lax.dot_general(
        left_side, right_side, (((0,), (0,)), ((), ())), preferred_element_type=F32
    )


def matmul_nt(left_side, right_side):
    return lax.dot_general(
        left_side, right_side, (((1,), (1,)), ((), ())), preferred_element_type=F32
    )


def stage_list(swap):
    dp_bits = lax.axis_size("dp").bit_length() - 1
    seq_bits = lax.axis_size("seq").bit_length() - 1
    rest = list(range(1, dp_bits))
    if swap:
        rest.reverse()
    order = [("dp", bit) for bit in [0] + rest]
    return order + [("seq", bit) for bit in range(seq_bits)], dp_bits, seq_bits


def stage_place(stage, dp_bits, seq_bits):
    axis, bit = stage
    return dp_bits - 1 - bit if axis == "dp" else dp_bits + seq_bits - 1 - bit


def my_bit(stage):
    axis, bit = stage
    return (lax.axis_index(axis) >> bit) & 1


def swap_halves(block, stage):
    axis, bit = stage
    pairs = [(i, i ^ (1 << bit)) for i in range(lax.axis_size(axis))]
    return lax.ppermute(block, axis, pairs)


def gather(shard, swap=False):
    stages, dp_bits, seq_bits = stage_list(swap)
    depth = dp_bits + seq_bits
    whole = (2,) * depth + shard.shape
    starts = [None] * depth
    for stage in stages:
        starts[stage_place(stage, dp_bits, seq_bits)] = my_bit(stage)
    starts += [0] * shard.ndim
    sizes = [1] * depth + list(shard.shape)
    buffer = jnp.zeros(whole, shard.dtype)
    block = shard.reshape(sizes)
    buffer = lax.dynamic_update_slice(buffer, block, starts)
    for index, stage in enumerate(reversed(stages)):
        place = stage_place(stage, dp_bits, seq_bits)
        if index > 0:
            block = lax.dynamic_slice(buffer, starts, sizes)
        other = list(starts)
        other[place] = 1 - starts[place]
        buffer = lax.dynamic_update_slice(buffer, swap_halves(block, stage), other)
        starts[place] = 0
        sizes[place] = 2
    return buffer.reshape((-1,) + shard.shape[1:])


def scatter(total, swap=False):
    stages, dp_bits, seq_bits = stage_list(swap)
    depth = dp_bits + seq_bits
    block = total.reshape((2,) * depth + (total.shape[0] >> depth,) + total.shape[1:])
    for stage in stages:
        place = stage_place(stage, dp_bits, seq_bits)
        mine = my_bit(stage)
        sent = lax.dynamic_slice_in_dim(block, 1 - mine, 1, place)
        kept = lax.dynamic_slice_in_dim(block, mine, 1, place)
        got = swap_halves(sent, stage)
        block = (kept.astype(F32) + got.astype(F32)).astype(total.dtype)
    return block.reshape((-1,) + total.shape[1:]).astype(F32)


def gather_vectors(vectors):
    packed = gather(jnp.concatenate(vectors)[None])
    unpacked = []
    start = 0
    for member in vectors:
        extent = member.shape[0]
        unpacked.append(packed[:, start : start + extent].reshape(-1).astype(F32))
        start += extent
    return unpacked


def scatter_vectors(totals, group_size):
    packed = jnp.concatenate([total.reshape(group_size, -1) for total in totals], 1)
    owned = scatter(packed).reshape(-1)
    pieces = []
    start = 0
    for total in totals:
        extent = total.shape[0] // group_size
        pieces.append(owned[start : start + extent])
        start += extent
    return pieces


def exchange(blocks):
    size = lax.axis_size("seq")
    me = lax.axis_index("seq")
    groups = blocks.reshape((size, -1) + blocks.shape[1:])
    own = lax.dynamic_index_in_dim(groups, me, 0)
    out = lax.dynamic_update_index_in_dim(jnp.zeros_like(groups), own, me, 0)
    for shift in range(1, size):
        target = lax.rem(me + shift, size)
        source = lax.rem(me + size - shift, size)
        pairs = [(i, (i + shift) % size) for i in range(size)]
        got = lax.ppermute(lax.dynamic_index_in_dim(groups, target, 0), "seq", pairs)
        out = lax.dynamic_update_index_in_dim(out, got, source, 0)
    return out.reshape(blocks.shape)


def to_images(values):
    seq_size = lax.axis_size("seq")
    tail = values.shape[2:]
    swapped = exchange(values.reshape((-1,) + tail))
    by_source = jnp.swapaxes(swapped.reshape((seq_size, -1) + tail), 0, 1)
    return by_source.reshape((by_source.shape[0], seq_size * tail[0]) + tail[1:])


def to_tokens(values, like):
    seq_size = lax.axis_size("seq")
    tail = like.shape[2:]
    by_target = jnp.swapaxes(values.reshape((-1, seq_size) + tail), 0, 1)
    return exchange(by_target.reshape((-1,) + tail)).reshape(like.shape)


def forward_kernel(okay_ref, q_ref, k_ref, v_ref, out_ref, prob_ref):
    okay = okay_ref[0] > 0
    head = q_ref.shape[2] // 2
    parts = []
    for j in range(2):
        lanes = slice(j * head, (j + 1) * head)
        scores = matmul_nt(k_ref[0, :, lanes], q_ref[0, :, lanes])
        scores = jnp.where(okay, scores, MASKED)
        exp_scores = jnp.exp(scores - jnp.max(scores, 0, keepdims=True))
        scale = 1.0 / jnp.sum(exp_scores, 0, keepdims=True)
        probs = (exp_scores * scale).astype(BF16)
        prob_ref[0, j] = probs
        parts.append(matmul_tn(v_ref[0, :, lanes], probs))
    out_ref[0] = jnp.concatenate(parts, 0).T.astype(BF16)


def backward_kernel(q_ref, k_ref, v_ref, prob_ref, go_ref, gq_ref, gk_ref, gv_ref):
    head = q_ref.shape[2] // 2
    scale = head ** (-0.5)
    parts = []
    for j in range(2):
        lanes = slice(j * head, (j + 1) * head)
        go = go_ref[0, :, lanes]
        probs = prob_ref[0, j]
        exact = probs.astype(F32)
        grad_probs = matmul_nt(v_ref[0, :, lanes], go)
        inner = jnp.sum(exact * grad_probs, 0, keepdims=True)
        grad_scores = (exact * (grad_probs - inner)).astype(BF16)
        parts.append(matmul_tn(k_ref[0, :, lanes], grad_scores))
        gk_ref[0, :, lanes] = matmul(grad_scores, q_ref[0, :, lanes]).astype(BF16)
        gv_ref[0, :, lanes] = matmul(probs, go).astype(BF16)
    gq_ref[0] = (jnp.concatenate(parts, 0).T.astype(BF16) * scale).astype(BF16)


def column_spec(extent, lanes, offset):
    return pl.BlockSpec((1, extent, lanes), lambda i, h: (i, 0, h + offset))


def attention_forward(mixed, okay):
    images, extent, triple = mixed.shape
    width = triple // 3
    lanes = 2 * width // HEADS
    pairs = HEADS // 2
    elements = images * HEADS * extent * extent
    return pl.pallas_call(
        forward_kernel,
        grid=(images, pairs),
        in_specs=[
            pl.BlockSpec((1, extent, 1), lambda i, h: (i, 0, 0)),
            column_spec(extent, lanes, 0),
            column_spec(extent, lanes, pairs),
            column_spec(extent, lanes, 2 * pairs),
        ],
        out_specs=[
            column_spec(extent, lanes, 0),
            pl.BlockSpec((1, 2, extent, extent), lambda i, h: (i, h, 0, 0)),
        ],
        out_shape=[
            jax.ShapeDtypeStruct((images, extent, width), BF16),
            jax.ShapeDtypeStruct((images, HEADS, extent, extent), BF16),
        ],
        compiler_params=pltpu.CompilerParams(vmem_limit_bytes=40 * 1024 * 1024),
        cost_estimate=pl.CostEstimate(
            flops=4 * elements * lanes // 2,
            bytes_accessed=2 * elements + 8 * images * extent * width,
            transcendentals=elements,
        ),
    )(okay[..., None].astype(F32), mixed, mixed, mixed)


def attention_backward(mixed, probs, grads):
    images, extent, triple = mixed.shape
    width = triple // 3
    lanes = 2 * width // HEADS
    pairs = HEADS // 2
    elements = images * HEADS * extent * extent
    gq, gk, gv = pl.pallas_call(
        backward_kernel,
        grid=(images, pairs),
        in_specs=[
            column_spec(extent, lanes, 0),
            column_spec(extent, lanes, pairs),
            column_spec(extent, lanes, 2 * pairs),
            pl.BlockSpec((1, 2, extent, extent), lambda i, h: (i, h, 0, 0)),
            column_spec(extent, lanes, 0),
        ],
        out_specs=[column_spec(extent, lanes, 0)] * 3,
        out_shape=[jax.ShapeDtypeStruct((images, extent, width), BF16)] * 3,
        compiler_params=pltpu.CompilerParams(vmem_limit_bytes=40 * 1024 * 1024),
        cost_estimate=pl.CostEstimate(
            flops=8 * elements * lanes // 2,
            bytes_accessed=2 * elements + 14 * images * extent * width,
            transcendentals=0,
        ),
    )(mixed, mixed, mixed, probs, grads)
    shape = (images * extent, width)
    return gq.reshape(shape), gk.reshape(shape), gv.reshape(shape)


def on_device(
    tokens,
    pad_mask,
    image_counts,
    cotangent,
    gain_one,
    shift_one,
    qkv_weight,
    query_bias,
    value_bias,
    out_weight,
    out_bias,
    gain_two,
    shift_two,
    up_weight,
    up_bias,
    down_weight,
    down_bias,
):
    micro_count, slot_count, local_len, width = tokens.shape
    seq_size = lax.axis_size("seq")
    group_size = lax.axis_size(BOTH)
    images = micro_count * slot_count // seq_size
    extent = local_len * seq_size
    rows = images * extent
    query_scale = (width // HEADS) ** (-0.5)

    vectors = gather_vectors(
        [
            gain_one,
            shift_one,
            query_bias,
            value_bias,
            out_bias,
            gain_two,
            shift_two,
            up_bias,
            down_bias,
        ]
    )
    gain1, shift1, qbias, vbias, obias, gain2, shift2, ubias, dbias = vectors
    mix_full = gather(qkv_weight)
    proj_full = gather(out_weight, True)
    up_full = gather(up_weight, True)
    down_full = gather(down_weight)

    image_okay = to_images(pad_mask)
    image_rows = to_images(tokens)
    image_grad = to_images(cotangent)

    place = lax.axis_index("seq") * images + jnp.arange(images)
    counts = image_counts[place // slot_count, 0]
    live = (image_okay > 0) & ((place % slot_count) < counts)[:, None]

    x = image_rows.reshape(rows, width).astype(F32)
    unit1, inverse1 = norm_stats(x)
    h1 = (unit1 * gain1 + shift1).astype(BF16)
    mixed_bias = jnp.concatenate([qbias, jnp.zeros_like(qbias), vbias])
    mixed_scale = jnp.where(jnp.arange(3 * width) < width, query_scale, 1.0)
    mixed = ((matmul(h1, mix_full) + mixed_bias) * mixed_scale).astype(BF16)
    per_image = (images, extent, width)
    mixed = mixed.reshape(images, extent, 3 * width)
    attended, probs = attention_forward(mixed, image_okay)
    attended = attended.reshape(rows, width)
    middle = x + (matmul(attended, proj_full) + obias)
    unit2, inverse2 = norm_stats(middle)
    h2 = (unit2 * gain2 + shift2).astype(BF16)
    pre_act = matmul(h2, up_full) + ubias
    hidden = jax.nn.gelu(pre_act, approximate=False).astype(BF16)
    result = (middle + (matmul(hidden, down_full) + dbias)).astype(BF16)
    block_out = to_tokens(result.reshape(per_image), tokens)

    c = jnp.where(live[..., None], image_grad, jnp.zeros_like(image_grad)).reshape(rows, width)
    w_down, c = lax.optimization_barrier((matmul_tn(hidden, c).astype(BF16), c))
    d_down = scatter(w_down)
    d_dbias = jnp.sum(c.astype(F32), 0)
    gelu_slope = jax.vjp(lambda u: jax.nn.gelu(u, approximate=False), pre_act)[1]
    du = gelu_slope(matmul_nt(c, down_full))[0].astype(BF16)
    w_up, du = lax.optimization_barrier((matmul_tn(h2, du).astype(BF16), du))
    d_up = scatter(w_up, True)
    d_ubias = jnp.sum(du.astype(F32), 0)
    g2 = matmul_nt(du, up_full)
    d_gain2 = jnp.sum(g2 * unit2, 0)
    d_shift2 = jnp.sum(g2, 0)
    gx2 = c.astype(F32) + norm_back(g2, gain2, unit2, inverse2)
    ga = gx2.astype(BF16)
    w_out, ga = lax.optimization_barrier((matmul_tn(attended, ga).astype(BF16), ga))
    d_out = scatter(w_out)
    d_obias = jnp.sum(ga.astype(F32), 0)
    go = matmul_nt(ga, proj_full).astype(BF16).reshape(per_image)
    gq, gk, gv = attention_backward(mixed, probs, go)
    gz = jnp.concatenate([gq, gk, gv], 1)
    w_mix, gz = lax.optimization_barrier((matmul_tn(h1, gz).astype(BF16), gz))
    near = 3 * width // 2
    d_mix = jnp.concatenate([scatter(w_mix[:, :near]), scatter(w_mix[:, near:], True)], 1)
    d_qbias = jnp.sum(gq.astype(F32), 0)
    d_vbias = jnp.sum(gv.astype(F32), 0)
    g1 = matmul_nt(gz, mix_full)
    d_gain1 = jnp.sum(g1 * unit1, 0)
    d_shift1 = jnp.sum(g1, 0)
    gx = gx2 + norm_back(g1, gain1, unit1, inverse1)
    grad_tokens = to_tokens(gx.astype(BF16).reshape(per_image), tokens).astype(F32)
    small = scatter_vectors(
        [
            d_gain1,
            d_shift1,
            d_qbias,
            d_vbias,
            d_obias,
            d_gain2,
            d_shift2,
            d_ubias,
            d_dbias,
        ],
        group_size,
    )
    return (
        block_out,
        grad_tokens,
        small[0],
        small[1],
        d_mix,
        small[2],
        small[3],
        d_out,
        small[4],
        small[5],
        small[6],
        d_up,
        small[7],
        d_down,
        small[8],
    )


def solution(mesh):
    image_spec = P(None, "dp", "seq", None)
    vector = P(BOTH)
    matrix = P(BOTH, None)
    params = (
        vector,
        vector,
        matrix,
        vector,
        vector,
        matrix,
        vector,
        vector,
        vector,
        matrix,
        vector,
        matrix,
        vector,
    )
    return jax.shard_map(
        on_device,
        mesh=mesh,
        in_specs=(image_spec, P(None, "dp", "seq"), P(None, "dp"), image_spec) + params,
        out_specs=(image_spec, image_spec) + params,
        check_vma=False,
    )
```
